32 devices in a mesh: dp: 2 (over x), mp: 16 (over z, y, core).
Axes of the slice: x: 2, y: 2, z: 4, core: 2. Of those that a mesh axis runs over, the one named last changes fastest.
Arguments:
- hidden_in: bfloat16 [1024, 8192], P('dp', 'mp'), may hold values from -6 to 6
- queries: bfloat16 [1024, 8192], P('dp', 'mp'), may hold values from -100 to 100
- key_rows: bfloat16 [1024, 1024], P('dp'), may hold values from -5.5 to 5.5
- value_rows: bfloat16 [1024, 1024], P('dp'), may hold values from -6 to 6
- teacher_proj: bfloat16 [8192, 8192], P('mp'), may hold values from -0.0625 to 0.0625
- mixer_in: bfloat16 [2, 8192, 8192], P(None, 'dp', 'mp'), may hold values from -0.0625 to 0.0625
- shared_in: bfloat16 [8192, 384], P('mp'), may hold values from -0.0625 to 0.0625
- dt_bias: float32 [128], P('mp'), may hold values from -3 to 1
- a_log: float32 [128], P('mp'), may hold values from -6.9 to 0
- d_skip: float32 [128], P('mp'), may hold values from 0.5 to 1.5
- norm_gain: float32 [8192], P('mp'), may hold values from 0.1 to 1.9
- mixer_out: bfloat16 [8192, 8192], P('mp'), may hold values from -0.0625 to 0.0625
Outputs:
- misfit: bfloat16 [1024, 8192], P(('dp', 'mp'))
The draws below stay inside these ranges and needn't reach their ends.
All inputs are finite; a program needn't handle non-finite values.
Results may differ from the reference program's by a relative error of at most 0.0051.
Values may be sent and summed in bfloat16 or wider, within the bound.
No kernel may reach another device: no remote copies, remote signals or barrier semaphores. Data moves between devices by JAX's collectives and lax.ppermute only.
A program may use at most 192 MiB of HBM per device.

```python
import jax
import jax.numpy as jnp
from jax import lax

D = 8192
QHEADS = 64
KVHEADS = 8
HEAD = 128
SHEADS = 128
SHEAD = 64
STATE = 128
LEN = 512
TOKENS = 1024
N_MP = 16


def attention_pair(key):
    base_keys = jnp.clip(jax.random.normal(key, (TOKENS, KVHEADS * HEAD), jnp.float32), -5.0, 5.0)
    base_queries = jnp.clip(jax.random.normal(jax.random.fold_in(key, 1), (TOKENS, QHEADS * HEAD), jnp.float32), -5.0, 5.0)
    key_out = base_keys
    query_out = base_queries
    return (query_out, key_out)


def draw_queries(key, part):
    query_out, key_out = attention_pair(key)
    return query_out.astype(jnp.bfloat16)


def draw_key_rows(key, part):
    query_out, key_out = attention_pair(key)
    return key_out.astype(jnp.bfloat16)


def block_scale(key, extent, split, least, top_value):
    def one(dim, parts):
        steps = jax.random.uniform(jax.random.fold_in(jax.random.fold_in(key, 6), dim), (parts,), jnp.float32, least / len(split), top_value / len(split))
        return jnp.repeat(jnp.exp(steps), extent[dim] // parts).reshape((-1,) + (1,) * (len(extent) - dim - 1))

    level = one(*split[0])
    for cut in split[1:]:
        level = level * one(*cut)
    return level


def noise(rng, shape, deviation, most, cuts=(), dtype=jnp.bfloat16):
    gain = block_scale(rng, shape, cuts, -0.22, 0.18) if cuts else 1.0
    values = jax.random.normal(rng, shape, jnp.float32) * deviation * gain
    return jnp.minimum(jnp.maximum(values, -most), most).astype(dtype)


def setup_inputs(seed: int = 0) -> dict:
    streams_of = jax.random.split(jax.random.key(seed), 13)
    return {
        "hidden_in": noise(streams_of[0], (TOKENS, D), 1.0, 6.0, ((0, 2), (1, 16))),
        "queries": draw_queries(jax.random.fold_in(streams_of[12], 71), 0),
        "key_rows": draw_key_rows(jax.random.fold_in(streams_of[12], 71), 0),
        "value_rows": noise(streams_of[3], (TOKENS, KVHEADS * HEAD), 1.0, 6.0, ((0, 2),)),
        "teacher_proj": noise(streams_of[4], (QHEADS * HEAD, D), (QHEADS * HEAD) ** -0.5, 0.0625, ((0, 16),)),
        "mixer_in": noise(streams_of[5], (2, D, SHEADS * SHEAD), D ** -0.5, 0.0625, ((1, 2), (2, 16))),
        "shared_in": noise(streams_of[6], (D, 2 * STATE + SHEADS), D ** -0.5, 0.0625, ((0, 16),)),
        "dt_bias": jnp.clip(-3.0 + 4.0 * jax.random.uniform(streams_of[7], (SHEADS,), jnp.float32) ** block_scale(streams_of[7], (SHEADS,), ((0, 16),), -0.2, 0.2), -3.0, 1.0),
        "a_log": jnp.clip(-6.9 + 6.9 * jax.random.uniform(streams_of[8], (SHEADS,), jnp.float32) ** block_scale(streams_of[8], (SHEADS,), ((0, 16),), -0.2, 0.2), -6.9, 0.0),
        "d_skip": jnp.clip(0.5 + 1.0 * jax.random.uniform(streams_of[9], (SHEADS,), jnp.float32) ** block_scale(streams_of[9], (SHEADS,), ((0, 16),), -0.2, 0.2), 0.5, 1.5),
        "norm_gain": jnp.clip(1.0 + 0.18 * jax.random.normal(streams_of[10], (SHEADS * SHEAD,), jnp.float32), 0.1, 1.9),
        "mixer_out": noise(streams_of[11], (SHEADS * SHEAD, D), (SHEADS * SHEAD) ** -0.5, 0.0625, ((0, 16),)),
    }


norm_eps = 1e-05

def student_normed(hidden_seq, mixer_in, shared_in, dt_bias, a_log, d_skip, norm_gain):
    scanned = jnp.dot(hidden_seq, mixer_in[0], preferred_element_type=jnp.float32)
    gate_in = jnp.dot(hidden_seq, mixer_in[1], preferred_element_type=jnp.float32)
    shared = jnp.dot(hidden_seq, shared_in, preferred_element_type=jnp.float32)
    b_in = shared[:, :STATE]
    c_out = shared[:, STATE:2 * STATE]
    dt_raw = shared[:, 2 * STATE:]
    step_size = jax.nn.softplus(dt_raw + dt_bias)
    log_decay = -step_size * jnp.exp(a_log)
    running = jnp.cumsum(log_decay, axis=0)
    contact = jnp.dot(c_out, b_in.T, precision=lax.Precision.HIGHEST)
    causal = jnp.arange(LEN)[:, None] >= jnp.arange(LEN)[None, :]

    def head_output(items):
        running_head, step_head, x_head = items
        spans = running_head[:, None] - running_head[None, :]
        weight = contact * jnp.exp(jnp.where(causal, spans, -jnp.inf)) * step_head[None, :]
        return jnp.dot(weight, x_head, precision=lax.Precision.HIGHEST)
    x_heads = scanned.reshape(LEN, SHEADS, SHEAD)
    outputs = lax.map(head_output, (running.T, step_size.T, x_heads.transpose(1, 0, 2)))
    ssd_out = outputs.transpose(1, 0, 2) + d_skip[None, :, None] * x_heads
    gated = ssd_out.reshape(LEN, SHEADS * SHEAD) * jax.nn.silu(gate_in)
    mean_square = lax.optimization_barrier(jnp.mean(gated * gated, axis=1, keepdims=True))
    return (gated * lax.rsqrt(mean_square + norm_eps) * norm_gain).astype(jnp.bfloat16)

def teacher_context(query_seq, key_seq, value_seq):
    group_size = QHEADS // KVHEADS
    query_heads = query_seq.astype(jnp.float32).reshape(LEN, QHEADS, HEAD)
    key_heads = jnp.repeat(key_seq.astype(jnp.float32).reshape(LEN, KVHEADS, HEAD), group_size, axis=1)
    value_heads = jnp.repeat(value_seq.astype(jnp.float32).reshape(LEN, KVHEADS, HEAD), group_size, axis=1)
    scores = jnp.einsum('thd,shd->hts', query_heads, key_heads) * HEAD ** (-0.5)
    causal = jnp.arange(LEN)[:, None] >= jnp.arange(LEN)[None, :]
    attn_probs = jax.nn.softmax(jnp.where(causal[None], scores, -jnp.inf), axis=-1).astype(jnp.bfloat16)
    context = jnp.einsum('hts,shd->thd', attn_probs.astype(jnp.float32), value_heads)
    return context.astype(jnp.bfloat16).reshape(LEN, QHEADS * HEAD)

def reference(hidden_in, queries, key_rows, value_rows, teacher_proj, mixer_in, shared_in, dt_bias, a_log, d_skip, norm_gain, mixer_out):
    sequences = TOKENS // LEN
    student_cols = SHEADS * SHEAD // N_MP
    teacher_cols = QHEADS * HEAD // N_MP

    def one_sequence(items):
        hidden_seq, query_seq, key_seq, value_seq = items
        normed = student_normed(hidden_seq, mixer_in, shared_in, dt_bias, a_log, d_skip, norm_gain)
        context = teacher_context(query_seq, key_seq, value_seq)
        normed_blocks = normed.reshape(LEN, N_MP, student_cols).transpose(1, 0, 2)
        context_blocks = context.reshape(LEN, N_MP, teacher_cols).transpose(1, 0, 2)
        mixer_blocks = mixer_out.reshape(N_MP, student_cols, D)
        proj_blocks = teacher_proj.reshape(N_MP, teacher_cols, D)

        def add_block(total, block):
            normed_b, context_b, mixer_b, proj_b = block
            term = jnp.dot(normed_b, mixer_b, preferred_element_type=jnp.float32) - jnp.dot(context_b, proj_b, preferred_element_type=jnp.float32)
            return (total + term, None)
        total, unused = lax.scan(add_block, jnp.zeros((LEN, D), jnp.float32), (normed_blocks, context_blocks, mixer_blocks, proj_blocks))
        return total
    mismatch = lax.map(one_sequence, (hidden_in.reshape(sequences, LEN, D), queries.reshape(sequences, LEN, QHEADS * HEAD), key_rows.reshape(sequences, LEN, KVHEADS * HEAD), value_rows.reshape(sequences, LEN, KVHEADS * HEAD))).reshape(TOKENS, D)
    return mismatch.astype(jnp.bfloat16)
```

```python
import functools

import jax
import jax.numpy as jnp
from jax import lax
from jax.experimental import pallas as pl
from jax.experimental.pallas import tpu as pltpu
from jax.sharding import PartitionSpec as P

HEAD = 128
SHEAD = 64
STATE = 128
LANES = 128
OUT_CHUNKS = 4
OUT_TILE = 512
VMEM = 56 * 1024 * 1024

norm_eps = 1e-05
f32 = jnp.float32
bf16 = jnp.bfloat16


def cost(flops, moved):
    return pl.CostEstimate(flops=flops, bytes_accessed=moved, transcendentals=0)


def pick(parts, index):
    chosen = parts[0]
    for m in range(1, len(parts)):
        chosen = jnp.where(index == m, parts[m], chosen)
    return chosen


def reorder_weights(mixer_in, block, spot):
    kinds, rows, channels = mixer_in.shape

    def body(spot_ref, source, target):
        target[...] = source[0]

    return pl.pallas_call(
        body,
        grid_spec=pltpu.PrefetchScalarGridSpec(
            num_scalar_prefetch=1,
            grid=(rows // block, kinds),
            in_specs=[pl.BlockSpec((1, block, channels), lambda r, k, s: (k, s[0] ^ r, 0))],
            out_specs=pl.BlockSpec((block, channels), lambda r, k, s: (r, k)),
        ),
        out_shape=jax.ShapeDtypeStruct((rows, kinds * channels), mixer_in.dtype),
        cost_estimate=cost(0, 4 * mixer_in.size),
        name="reorder_weights",
    )(spot, mixer_in)


def scan_weights(n, rows, b_in, c_out, run_col, run_row, step_row):
    heads = run_row.shape[0]
    pairs = heads // 2
    wide = 2 * rows

    def body(b_ref, c_ref, col_ref, row_ref, step_ref, out_ref):
        below = lax.broadcasted_iota(jnp.int32, (rows, rows), 0) >= lax.broadcasted_iota(
            jnp.int32, (rows, rows), 1
        )
        for j in range(n + 1):
            contact = lax.dot_general(
                c_ref[...],
                b_ref[j * rows : (j + 1) * rows],
                (((1,), (1,)), ((), ())),
                precision=lax.Precision.HIGHEST,
                preferred_element_type=f32,
            )
            for h in range(heads):
                span = col_ref[:, h : h + 1] - row_ref[j, h : h + 1, :]
                if j == n:
                    span = jnp.where(below, span, -jnp.inf)
                weight = contact * jnp.exp(span) * step_ref[j, h : h + 1, :]
                high = weight.astype(bf16)
                low = (weight - high.astype(f32)).astype(bf16)
                at = (h % 2) * rows
                out_ref[h // 2, at : at + rows, j * wide : (j + 1) * wide] = jnp.concatenate(
                    [high, low], axis=1
                )

    grown = (n + 1) * rows
    by_chunk = lambda a: a[:, :grown].reshape(heads, n + 1, rows).transpose(1, 0, 2)
    return pl.pallas_call(
        body,
        out_shape=jax.ShapeDtypeStruct((pairs, wide, (n + 1) * wide), bf16),
        compiler_params=pltpu.CompilerParams(vmem_limit_bytes=VMEM),
        cost_estimate=cost(12 * grown * rows * STATE, 4 * heads * grown * rows),
        name="scan_weights",
    )(
        b_in[:grown],
        c_out[n * rows : grown],
        run_col[n * rows : grown],
        by_chunk(run_row),
        by_chunk(step_row),
    )


def scan_chunk(n, rows, weights, own, others, earlier, skip, gain):
    pairs, wide, _ = weights.shape
    channels = skip.shape[1]

    def body(*refs):
        weights_ref, own_ref, skip_ref, gain_ref = refs[:4]
        other_refs = refs[4 : 4 + len(others)]
        earlier_refs = refs[4 + len(others) : 4 + len(others) + n]
        split_ref, gated_ref, squares_ref = refs[4 + len(others) + n :]
        left = lax.broadcasted_iota(jnp.int32, (rows, LANES), 1) < SHEAD
        squares = jnp.zeros((rows, 1), f32)
        for p in range(pairs):
            lane = slice(p * LANES, (p + 1) * LANES)
            gate_lane = slice(channels + p * LANES, channels + (p + 1) * LANES)
            x = own_ref[:, lane]
            gate = own_ref[:, gate_lane]
            for other in other_refs:
                x = x + other[:, lane].astype(f32)
                gate = gate + other[:, gate_lane].astype(f32)
            high = x.astype(bf16)
            low = (x - high.astype(f32)).astype(bf16)
            both = jnp.concatenate([high, low], axis=1)
            split_ref[p] = jnp.concatenate([both, both], axis=0)
            total = jnp.dot(
                weights_ref[p, :, n * wide : (n + 1) * wide],
                split_ref[p],
                preferred_element_type=f32,
            )
            for j in range(n):
                total = total + jnp.dot(
                    weights_ref[p, :, j * wide : (j + 1) * wide],
                    earlier_refs[j][p],
                    preferred_element_type=f32,
                )
            total = total[:, :LANES] + total[:, LANES:]
            scanned = jnp.where(left, total[:rows], total[rows:])
            gated = (scanned + skip_ref[:, lane] * x) * (gate / (1.0 + jnp.exp(-gate)))
            squares = squares + jnp.sum(gated * gated, axis=1, keepdims=True)
            gated_ref[:, lane] = (gated * gain_ref[:, lane]).astype(bf16)
        squares_ref[...] = squares

    return pl.pallas_call(
        body,
        out_shape=(
            jax.ShapeDtypeStruct((pairs, wide, 2 * LANES), bf16),
            jax.ShapeDtypeStruct((rows, channels), bf16),
            jax.ShapeDtypeStruct((rows, 1), f32),
        ),
        compiler_params=pltpu.CompilerParams(vmem_limit_bytes=VMEM),
        cost_estimate=cost(2 * pairs * wide * wide * 2 * LANES * (n + 1), 8 * rows * channels * 2),
        name="scan_chunk",
    )(weights, own, skip, gain, *others, *earlier)


def project_out(n, width, spots, gated, gated_other, weight, weight_other, scale, teacher):
    length, channels = gated.shape
    half = weight_other.shape[1]
    far = scale.shape[0]
    tile = min(OUT_TILE, width)
    steps = width // tile
    part = length // (2 * far)

    def body(spot_ref, g_ref, go_ref, w_ref, wo_ref, r_ref, t_ref, keep_ref, send_ref):
        z, y = spot_ref[0], spot_ref[1]
        value = jnp.dot(g_ref[...], w_ref[...], preferred_element_type=f32) + jnp.dot(
            go_ref[...], wo_ref[...], preferred_element_type=f32
        )
        value = value.reshape(far, 2, part, tile)
        for zt in range(far):
            near = value[zt, 0] * r_ref[zt, 0] - t_ref[zt, 0]
            away = value[zt, 1] * r_ref[zt, 1] - t_ref[zt, 1]
            keep_ref[zt ^ z] = jnp.where(y == 0, near, away)
            send_ref[zt ^ z] = jnp.where(y == 0, away, near).astype(bf16)

    return pl.pallas_call(
        body,
        grid_spec=pltpu.PrefetchScalarGridSpec(
            num_scalar_prefetch=1,
            grid=(steps,),
            in_specs=[
                pl.BlockSpec((length, channels), lambda t, s: (0, 0)),
                pl.BlockSpec((length, channels), lambda t, s: (0, 0)),
                pl.BlockSpec(
                    (channels, tile), lambda t, s: (0, s[2] * (half // tile) + n * steps + t)
                ),
                pl.BlockSpec((channels, tile), lambda t, s: (0, n * steps + t)),
                pl.BlockSpec((far, 2, part, 1), lambda t, s: (0, 0, 0, 0)),
                pl.BlockSpec((far, 2, part, tile), lambda t, s: (0, 0, 0, n * steps + t)),
            ],
            out_specs=[
                pl.BlockSpec((far, part, tile), lambda t, s: (0, 0, t)),
                pl.BlockSpec((far, part, tile), lambda t, s: (0, 0, t)),
            ],
        ),
        out_shape=(
            jax.ShapeDtypeStruct((far, part, width), f32),
            jax.ShapeDtypeStruct((far, part, width), bf16),
        ),
        compiler_params=pltpu.CompilerParams(vmem_limit_bytes=VMEM),
        cost_estimate=cost(4 * length * channels * width, 8 * channels * width + 6 * length * width),
        name="project_out",
    )(spots, gated, gated_other, weight, weight_other, scale, teacher)


def add_near(keep, came):
    far, part, width = keep.shape

    def body(keep_ref, came_ref, *outs):
        for k in range(far):
            total = keep_ref[k] + came_ref[k].astype(f32)
            outs[k][...] = total.astype(outs[k].dtype)

    return pl.pallas_call(
        body,
        out_shape=tuple(
            jax.ShapeDtypeStruct((part, width), f32 if k == 0 else bf16) for k in range(far)
        ),
        compiler_params=pltpu.CompilerParams(vmem_limit_bytes=VMEM),
        cost_estimate=cost(keep.size, 8 * keep.size),
        name="add_near",
    )(keep, came)


def add_far(kept, came):
    def body(kept_ref, *refs):
        total = kept_ref[...]
        for ref in refs[:-1]:
            total = total + ref[...].astype(f32)
        refs[-1][...] = total.astype(bf16)

    return pl.pallas_call(
        body,
        out_shape=jax.ShapeDtypeStruct(kept.shape, bf16),
        cost_estimate=cost(kept.size, 12 * kept.size),
        name="add_far",
    )(kept, *came)


def local(
    ndp,
    nmp,
    hidden_in,
    queries,
    key_rows,
    value_rows,
    teacher_proj,
    mixer_in,
    shared_in,
    dt_bias,
    a_log,
    d_skip,
    norm_gain,
    mixer_out,
):
    far = nmp // 4
    group = far // ndp
    me = lax.axis_index("mp")
    seq = lax.axis_index("dp")
    core, y, z = me % 2, (me // 2) % 2, me // 4

    def swap(source, k):
        return lax.ppermute(source, "mp", [(s, s ^ k) for s in range(nmp)])

    def cross(source, k):
        return lax.ppermute(source, "dp", [(s, s ^ k) for s in range(ndp)])

    length, block = hidden_in.shape
    channels = mixer_in.shape[2]
    heads = dt_bias.shape[0]
    rows = length // far
    spots = jnp.stack([z, y, core]).astype(jnp.int32)

    def at(source, index):
        return lax.dynamic_index_in_dim(source, index, 0, False)

    part = jnp.dot(hidden_in, shared_in, preferred_element_type=f32)
    part = part.reshape(2, length // 2, -1)
    part = at(part, core) + swap(at(part, 1 - core), 1)
    part = part.reshape(2, length // 4, -1)
    part = at(part, y) + swap(at(part, 1 - y), 2)
    part = part.reshape(far, length // nmp, -1)
    share = at(part, z)
    for k in range(1, far):
        share = share + swap(at(part, z ^ k), 4 * k)
    shares = jnp.stack([share] + [swap(share, 4 * k) for k in range(1, far)])
    shared = jnp.concatenate([at(shares, m ^ z) for m in range(far)])
    came = swap(shared, 2)
    shared = jnp.concatenate([jnp.where(y == 0, shared, came), jnp.where(y == 0, came, shared)])
    came = swap(shared, 1)
    shared = jnp.concatenate(
        [jnp.where(core == 0, shared, came), jnp.where(core == 0, came, shared)]
    )

    turn = (z // group) ^ seq
    spot = (me % (4 * group)).astype(jnp.int32).reshape(1)
    weights_in = reorder_weights(mixer_in, block, spot)
    own_parts, other_parts = [], []
    for n in range(far):
        mine = hidden_in[n * rows : (n + 1) * rows]
        line = [mine] + [swap(mine, 4 * k) for k in range(1, far)]
        line = [jnp.stack(line[m * group : (m + 1) * group]) for m in range(ndp)]
        square = [pick(line, turn ^ d) for d in range(ndp)]
        square = jnp.stack([square[0]] + [cross(square[d], d) for d in range(1, ndp)], 1)
        both = [square, swap(square, 2)]
        all_four = [[q, swap(q, 1)] for q in both]
        features = jnp.concatenate(
            [all_four[b][c][k] for k in range(group) for b in range(2) for c in range(2)], axis=-1
        )
        projected = jnp.dot(
            features.reshape(ndp * rows, -1), weights_in, preferred_element_type=f32
        ).reshape(ndp, rows, -1)
        own_parts.append(projected[0])
        other_parts.append([cross(projected[d].astype(bf16), d) for d in range(1, ndp)])

    head_count = queries.shape[1] // HEAD
    query_heads_all = head_count * nmp
    kv_heads = key_rows.shape[1] // HEAD
    kv_head = me * head_count // (query_heads_all // kv_heads)
    key_sel = lax.dynamic_slice_in_dim(key_rows, kv_head * HEAD, HEAD, 1)
    value_sel = lax.dynamic_slice_in_dim(value_rows, kv_head * HEAD, HEAD, 1)
    query_heads = queries.reshape(length, head_count, HEAD)
    scores = jnp.einsum(
        "thd,sd->hts", query_heads, key_sel, preferred_element_type=f32
    ) * HEAD ** (-0.5)
    causal = jnp.arange(length)[:, None] >= jnp.arange(length)[None, :]
    attn_probs = jax.nn.softmax(jnp.where(causal[None], scores, -jnp.inf), axis=-1).astype(bf16)
    context = jnp.einsum("hts,sd->thd", attn_probs, value_sel, preferred_element_type=f32)
    context = context.astype(bf16).reshape(length, head_count * HEAD)

    half = mixer_out.shape[1] // 2

    def halves(weight):
        return lax.dynamic_slice_in_dim(weight, (1 - core) * half, half, 1)

    mixer_other = swap(halves(mixer_out), 1)
    teacher_other = swap(halves(teacher_proj), 1)
    teacher_own = lax.dynamic_slice_in_dim(teacher_proj, core * half, half, 1)
    teacher = jnp.dot(context, teacher_own, preferred_element_type=f32) + jnp.dot(
        swap(context, 1), teacher_other, preferred_element_type=f32
    )
    teacher = teacher.reshape(far, 2, rows // 2, half)

    b_in = shared[:, :STATE]
    c_out = shared[:, STATE : 2 * STATE]
    dt_raw = lax.dynamic_slice_in_dim(shared, 2 * STATE + me * heads, heads, 1)
    step_size = jax.nn.softplus(dt_raw + dt_bias)
    log_decay = -step_size * jnp.exp(a_log)
    running = jnp.dot(causal.astype(f32), log_decay, precision=lax.Precision.HIGHEST)
    run_row, step_row = running.T, step_size.T
    skip = jnp.repeat(d_skip, SHEAD)[None, :]
    earlier, gated, gated_other, squares = [], [], [], []
    for n in range(far):
        weights = scan_weights(n, rows, b_in, c_out, running, run_row, step_row)
        split, gated_n, squares_n = scan_chunk(
            n, rows, weights, own_parts[n], other_parts[n], earlier, skip, norm_gain[None, :]
        )
        earlier.append(split)
        gated.append(gated_n)
        gated_other.append(swap(gated_n, 1))
        squares.append(squares_n.reshape(1, rows))
    gated = jnp.concatenate(gated)
    gated_other = jnp.concatenate(gated_other)
    squares = jnp.concatenate(squares)
    k = 1
    while k < nmp:
        squares = squares + swap(squares, k)
        k *= 2
    scale = lax.rsqrt(squares / (channels * nmp) + norm_eps).reshape(far, 2, rows // 2, 1)

    width = half // OUT_CHUNKS
    done = []
    for n in range(OUT_CHUNKS):
        keep, send = project_out(
            n, width, spots, gated, gated_other, mixer_out, mixer_other, scale, teacher
        )
        sums = add_near(keep, swap(send, 2))
        done.append(add_far(sums[0], [swap(sums[k], 4 * k) for k in range(1, far)]))
    total = jnp.concatenate(done, axis=1).reshape(2, rows // 4, half)
    stay = at(total, core)
    came = swap(at(total, 1 - core), 1)
    return jnp.concatenate(
        [jnp.where(core == 0, stay, came), jnp.where(core == 0, came, stay)], axis=1
    )


def solution(mesh):
    placed = (
        P("dp", "mp"),
        P("dp", "mp"),
        P("dp", None),
        P("dp", None),
        P("mp", None),
        P(None, "dp", "mp"),
        P("mp", None),
        P("mp"),
        P("mp"),
        P("mp"),
        P("mp"),
        P("mp", None),
    )
    return jax.shard_map(
        functools.partial(local, mesh.shape["dp"], mesh.shape["mp"]),
        mesh=mesh,
        in_specs=placed,
        out_specs=P(("dp", "mp"), None),
        check_vma=False,
    )
```

```python
import functools

import jax
import jax.numpy as jnp
from jax import lax
from jax.experimental import pallas as pl
from jax.experimental.pallas import tpu as pltpu
from jax.sharding import PartitionSpec as P

HEAD = 128
SHEAD = 64
STATE = 128
LANES = 128
OUT_CHUNKS = 4
SPLIT = (2, 3, 3)
HINT = 16
OUT_TILE = 512
SMALL = 8 * 1024 * 1024
MIDDLE = 14 * 1024 * 1024
LARGE = 58 * 1024 * 1024

norm_eps = 1e-05
f32 = jnp.float32
bf16 = jnp.bfloat16


def cost(flops, moved):
    return pl.CostEstimate(flops=flops // HINT, bytes_accessed=moved // HINT, transcendentals=0)


def after(value, *events):
    return lax.optimization_barrier((value, *events))[0]


def pick(parts, index):
    chosen = parts[0]
    for m in range(1, len(parts)):
        chosen = jnp.where(index == m, parts[m], chosen)
    return chosen


def reorder_weights(mixer_in, block, spot):
    kinds, rows, channels = mixer_in.shape

    def body(spot_ref, source, target):
        for k in range(kinds):
            target[:, k * channels : (k + 1) * channels] = source[k]

    return pl.pallas_call(
        body,
        grid_spec=pltpu.PrefetchScalarGridSpec(
            num_scalar_prefetch=1,
            grid=(rows // block,),
            in_specs=[pl.BlockSpec((kinds, block, channels), lambda r, s: (0, s[0] ^ r, 0))],
            out_specs=pl.BlockSpec((block, kinds * channels), lambda r, s: (r, 0)),
        ),
        out_shape=jax.ShapeDtypeStruct((rows, kinds * channels), mixer_in.dtype),
        compiler_params=pltpu.CompilerParams(vmem_limit_bytes=SMALL),
        cost_estimate=cost(0, 4 * mixer_in.size),
        name="reorder_weights",
    )(spot, mixer_in)


def attention(queries, key_rows, value_rows, kv_head):
    length, columns = queries.shape
    heads = columns // HEAD
    tall = min(length, 128)

    def body(kv_ref, q_ref, k_ref, v_ref, out_ref):
        for r in range(length // tall):
            seen = (r + 1) * tall
            at = slice(r * tall, seen)
            scores = lax.dot_general(
                q_ref[at], k_ref[:seen], (((1,), (1,)), ((), ())), preferred_element_type=f32
            ) * HEAD ** (-0.5)
            row = lax.broadcasted_iota(jnp.int32, (tall, seen), 0) + r * tall
            column = lax.broadcasted_iota(jnp.int32, (tall, seen), 1)
            scores = jnp.where(row >= column, scores, -jnp.inf)
            grown = jnp.exp(scores - jnp.max(scores, axis=1, keepdims=True))
            probs = (grown / jnp.sum(grown, axis=1, keepdims=True)).astype(bf16)
            out_ref[at] = jnp.dot(probs, v_ref[:seen], preferred_element_type=f32).astype(bf16)

    return pl.pallas_call(
        body,
        grid_spec=pltpu.PrefetchScalarGridSpec(
            num_scalar_prefetch=1,
            grid=(heads,),
            in_specs=[
                pl.BlockSpec((length, HEAD), lambda h, s: (0, h)),
                pl.BlockSpec((length, HEAD), lambda h, s: (0, s[0])),
                pl.BlockSpec((length, HEAD), lambda h, s: (0, s[0])),
            ],
            out_specs=pl.BlockSpec((length, HEAD), lambda h, s: (0, h)),
        ),
        out_shape=jax.ShapeDtypeStruct((length, columns), bf16),
        compiler_params=pltpu.CompilerParams(vmem_limit_bytes=SMALL),
        cost_estimate=cost(4 * length * length * columns, 4 * length * columns),
        name="attention",
    )(kv_head, queries, key_rows, value_rows)


def scan_weights(n, rows, shared, run_col, run_row, step_row):
    heads = run_row.shape[0]
    pairs = heads // 2
    wide = 2 * rows
    here = slice(n * rows, (n + 1) * rows)

    def body(shared_ref, col_ref, row_ref, step_ref, out_ref):
        below = lax.broadcasted_iota(jnp.int32, (rows, rows), 0) >= lax.broadcasted_iota(
            jnp.int32, (rows, rows), 1
        )
        for j in range(n + 1):
            there = slice(j * rows, (j + 1) * rows)
            contact = lax.dot_general(
                shared_ref[here, STATE : 2 * STATE],
                shared_ref[there, :STATE],
                (((1,), (1,)), ((), ())),
                precision=lax.Precision.HIGHEST,
                preferred_element_type=f32,
            )
            for h in range(heads):
                span = col_ref[here, h : h + 1] - row_ref[h : h + 1, there]
                if j == n:
                    span = jnp.where(below, span, -jnp.inf)
                weight = contact * jnp.exp(span) * step_ref[h : h + 1, there]
                high = weight.astype(bf16)
                low = (weight - high.astype(f32)).astype(bf16)
                at = (h % 2) * rows
                out_ref[h // 2, at : at + rows, j * wide : (j + 1) * wide] = jnp.concatenate(
                    [high, low], axis=1
                )

    grown = (n + 1) * rows
    return pl.pallas_call(
        body,
        out_shape=jax.ShapeDtypeStruct((pairs, wide, (n + 1) * wide), bf16),
        compiler_params=pltpu.CompilerParams(vmem_limit_bytes=SMALL),
        cost_estimate=cost(12 * grown * rows * STATE, 4 * heads * grown * rows),
        name="scan_weights",
    )(shared, run_col, run_row, step_row)


def scan_chunk(n, rows, weights, pieces, earlier, skip, gain):
    pairs, wide, _ = weights.shape
    channels = skip.shape[1]
    parts = [a for a, _, _ in pieces]
    count = 3 + sum(map(len, parts))

    def body(*refs):
        weights_ref, skip_ref, gain_ref = refs[:3]
        earlier_refs = refs[count : count + n]
        split_ref, gated_ref, squares_ref = refs[count + n :]

        def projected(lane):
            found, at = [], 3
            for arrays, start, stop in pieces:
                total = refs[at][start:stop, lane]
                for m in range(1, len(arrays)):
                    total = total + refs[at + m][start:stop, lane].astype(f32)
                at += len(arrays)
                found.append(total)
            return jnp.concatenate(found, axis=0) if len(found) > 1 else found[0]

        left = lax.broadcasted_iota(jnp.int32, (rows, LANES), 1) < SHEAD
        squares = jnp.zeros((rows, LANES), f32)
        for p in range(pairs):
            lane = slice(p * LANES, (p + 1) * LANES)
            gate_lane = slice(channels + p * LANES, channels + (p + 1) * LANES)
            x = projected(lane)
            gate = projected(gate_lane)
            high = x.astype(bf16)
            low = (x - high.astype(f32)).astype(bf16)
            both = jnp.concatenate([high, low], axis=1)
            split_ref[p] = jnp.concatenate([both, both], axis=0)
            total = jnp.dot(
                weights_ref[p, :, n * wide : (n + 1) * wide],
                split_ref[p],
                preferred_element_type=f32,
            )
            for j in range(n):
                total = total + jnp.dot(
                    weights_ref[p, :, j * wide : (j + 1) * wide],
                    earlier_refs[j][p],
                    preferred_element_type=f32,
                )
            total = total[:, :LANES] + total[:, LANES:]
            scanned = jnp.where(left, total[:rows], total[rows:])
            gated = (scanned + skip_ref[:, lane] * x) * (gate / (1.0 + jnp.exp(-gate)))
            squares = squares + gated * gated
            gated_ref[:, lane] = (gated * gain_ref[:, lane]).astype(bf16)
        squares_ref[...] = lax.dot_general(
            jnp.ones((8, LANES), f32),
            squares,
            (((1,), (1,)), ((), ())),
            precision=lax.Precision.HIGHEST,
            preferred_element_type=f32,
        )[:1]

    return pl.pallas_call(
        body,
        out_shape=(
            jax.ShapeDtypeStruct((pairs, wide, 2 * LANES), bf16),
            jax.ShapeDtypeStruct((rows, channels), bf16),
            jax.ShapeDtypeStruct((1, rows), f32),
        ),
        compiler_params=pltpu.CompilerParams(vmem_limit_bytes=MIDDLE),
        cost_estimate=cost(2 * pairs * wide * wide * 2 * LANES * (n + 1), 8 * rows * channels * 2),
        name="scan_chunk",
    )(weights, skip, gain, *(a for arrays in parts for a in arrays), *earlier)


def project_out(at, width, spots, here, there, weight, weight_there, scale=None, *teacher):
    spots, far = spots
    sets = [(here, there)] + ([teacher[:2]] if teacher else [])
    weights = [weight, weight_there] + list(teacher[2:])
    pieces = [p for pair in sets for group in pair for p in group]
    channels = here[0].shape[1]
    length = sum(p.shape[0] for p in here)
    half = weight_there.shape[1]
    tile = min(OUT_TILE, width)
    steps = width // tile
    part = length // (2 * far)

    def body(spot_ref, *refs):
        weight_refs = refs[len(pieces) : len(pieces) + len(weights)]
        scale_ref = refs[len(pieces) + len(weights)]
        keep_ref, send_ref, rows_ref, tiles_ref, done = refs[-5:]
        z, y = spot_ref[0], spot_ref[1]
        own = pl.multiple_of(spot_ref[2] * half + at, LANES)
        copies = []
        for t in range(steps):
            for m, ref in enumerate(weight_refs):
                column = (own if m % 2 == 0 else at) + t * tile
                copies.append(
                    pltpu.make_async_copy(
                        ref.at[:, pl.ds(pl.multiple_of(column, LANES), tile)],
                        tiles_ref.at[t * len(weights) + m],
                        done.at[t * len(weights) + m],
                    )
                )
        for copy in copies:
            copy.start()
        from_row, slot = 0, 0
        for ref in refs[: len(pieces)]:
            size = ref.shape[0]
            rows_ref[slot, from_row : from_row + size] = ref[...]
            from_row += size
            if from_row == length:
                from_row, slot = 0, slot + 1
        for t in range(steps):
            lane = slice(t * tile, (t + 1) * tile)
            products = []
            for m in range(len(weights)):
                copies[t * len(weights) + m].wait()
            for m in range(0, len(weights), 2):
                first = t * len(weights) + m
                products.append(
                    jnp.dot(rows_ref[m], tiles_ref[first], preferred_element_type=f32)
                    + jnp.dot(rows_ref[m + 1], tiles_ref[first + 1], preferred_element_type=f32)
                )
            for zt in range(far):
                low = zt * 2 * part
                near, away = (
                    products[0][low + e * part : low + (e + 1) * part] for e in range(2)
                )
                if teacher:
                    near = near * scale_ref[zt, 0] - products[1][low : low + part]
                    away = away * scale_ref[zt, 1] - products[1][low + part : low + 2 * part]
                keep_ref[zt ^ z, :, lane] = jnp.where(y == 0, near, away)
                send_ref[zt ^ z, :, lane] = jnp.where(y == 0, away, near).astype(bf16)

    return pl.pallas_call(
        body,
        in_specs=[pl.BlockSpec(memory_space=pltpu.SMEM)]
        + [pl.BlockSpec(memory_space=pltpu.VMEM)] * len(pieces)
        + [pl.BlockSpec(memory_space=pltpu.HBM)] * len(weights)
        + ([pl.BlockSpec(memory_space=pltpu.VMEM)] if teacher else []),
        out_specs=[pl.BlockSpec(memory_space=pltpu.VMEM)] * 2,
        out_shape=(
            jax.ShapeDtypeStruct((far, part, width), f32),
            jax.ShapeDtypeStruct((far, part, width), bf16),
        ),
        scratch_shapes=[
            pltpu.VMEM((len(weights), length, channels), bf16),
            pltpu.VMEM((steps * len(weights), channels, tile), bf16),
            pltpu.SemaphoreType.DMA((steps * len(weights),)),
        ],
        compiler_params=pltpu.CompilerParams(vmem_limit_bytes=LARGE),
        cost_estimate=cost(
            2 * len(weights) * length * channels * width,
            2 * len(weights) * channels * width + 6 * length * width,
        ),
        name="project_out",
    )(spots, *pieces, *weights, *([scale] if teacher else []))


def add_near(keep, came, scale=None, teacher=None, teacher_came=None):
    far, part, width = keep.shape
    stay = far // 2
    extra = [a for a in (scale, teacher, teacher_came) if a is not None]

    def body(keep_ref, came_ref, *refs):
        stay_ref, send_ref = refs[-2:]
        for k in range(far):
            total = keep_ref[k] + came_ref[k].astype(f32)
            if extra:
                total = total * refs[0][k] - (refs[1][k] + refs[2][k].astype(f32))
            if k % 2 == 0:
                stay_ref[k // 2] = total
            else:
                send_ref[k // 2] = total.astype(bf16)

    return pl.pallas_call(
        body,
        out_shape=(
            jax.ShapeDtypeStruct((stay, part, width), f32),
            jax.ShapeDtypeStruct((stay, part, width), bf16),
        ),
        compiler_params=pltpu.CompilerParams(vmem_limit_bytes=SMALL),
        cost_estimate=cost(keep.size, 8 * keep.size),
        name="add_near",
    )(keep, came, *extra)


def finish(spots, kept, came):
    rows, width = kept[0].shape
    rows //= 2
    count = len(kept)

    def body(spot_ref, *refs):
        own_ref, other_ref = refs[-2:]
        core = spot_ref[2]
        for n in range(count):
            total = (refs[n][...] + refs[count + n][...].astype(f32)).astype(bf16)
            low, high = total[:rows], total[rows:]
            lane = slice(n * width, (n + 1) * width)
            own_ref[:, lane] = jnp.where(core == 0, low, high)
            other_ref[:, lane] = jnp.where(core == 0, high, low)

    return pl.pallas_call(
        body,
        in_specs=[pl.BlockSpec(memory_space=pltpu.SMEM)]
        + [pl.BlockSpec(memory_space=pltpu.VMEM)] * (2 * count),
        out_shape=(jax.ShapeDtypeStruct((rows, count * width), bf16),) * 2,
        compiler_params=pltpu.CompilerParams(vmem_limit_bytes=SMALL),
        cost_estimate=cost(kept[0].size * count, 8 * kept[0].size * count),
        name="finish",
    )(spots, *kept, *came)


def local(
    ndp,
    nmp,
    hidden_in,
    queries,
    key_rows,
    value_rows,
    teacher_proj,
    mixer_in,
    shared_in,
    dt_bias,
    a_log,
    d_skip,
    norm_gain,
    mixer_out,
):
    far = nmp // 4
    group = far // ndp
    me = lax.axis_index("mp")
    seq = lax.axis_index("dp")
    core, y, z = me % 2, (me // 2) % 2, me // 4

    def swap(source, k):
        return lax.ppermute(source, "mp", [(s, s ^ k) for s in range(nmp)])

    def cross(source, k):
        return lax.ppermute(source, "dp", [(s, s ^ k) for s in range(ndp)])

    length, block = hidden_in.shape
    channels = mixer_in.shape[2]
    heads = dt_bias.shape[0]
    rows = length // far
    spots = jnp.stack([z, y, core]).astype(jnp.int32)

    def at(source, index):
        return lax.dynamic_index_in_dim(source, index, 0, False)

    head_count = queries.shape[1] // HEAD
    kv_heads = key_rows.shape[1] // HEAD
    kv_head = (me * head_count // (head_count * nmp // kv_heads)).astype(jnp.int32).reshape(1)
    context = attention(queries, key_rows, value_rows, kv_head)

    shared = lax.psum(jnp.dot(hidden_in, shared_in, preferred_element_type=f32), "mp")

    turn = (z // group) ^ seq
    spot = (me % (4 * group)).astype(jnp.int32).reshape(1)
    distances = [0]
    k = far // 2
    while k:
        distances += [d + k for d in distances]
        k //= 2
    order = [distances.index(d) for d in range(far)]
    sizes = [length * share // sum(SPLIT) for share in SPLIT]
    ends = [sum(sizes[: n + 1]) for n in range(len(sizes))]
    before = {}

    def in_turn(step, value):
        return after(value, before[step]) if step in before else value

    half = mixer_out.shape[1] // 2
    width = half // OUT_CHUNKS

    def half_sent(weight):
        return lax.dynamic_slice_in_dim(weight, (1 - core) * half, half, 1)

    weights_in = None
    projected = []
    for n, size in enumerate(sizes):
        line = [hidden_in[ends[n] - size : ends[n]]]
        k = far // 2
        while k:
            packed = in_turn(k, jnp.stack(line))
            if n == 0 and k == 1:
                packed = after(packed, context)
            came = before[k] = swap(packed, 4 * k)
            line = line + [came[m] for m in range(len(line))]
            k //= 2
        line = [line[m] for m in order]
        line = [jnp.stack(line[m * group : (m + 1) * group]) for m in range(ndp)]
        square = [pick(line, turn ^ d) for d in range(ndp)]
        away = in_turn("dp", tuple(square[1:]))
        square = before["dp"] = jnp.stack(
            [square[0]] + [cross(away[d - 1], d) for d in range(1, ndp)], 1
        )
        if weights_in is None:
            weights_in = reorder_weights(after(mixer_in, line[0]), block, spot)
        if n == 0:
            sent = [half_sent(after(weight, square)) for weight in (teacher_proj, mixer_out)]
        if n == 1:
            square = after(square, *sent)
            teacher_there, mixer_there = (swap(weight, 1) for weight in sent)
            teacher = ([context], [swap(context, 1)], teacher_proj, teacher_there)
            first = project_out(0, width, (spots, far), *teacher)
        if n == len(sizes) - 1:
            square = after(square, first[1])
        both = jnp.stack([square, swap(square, 2)])
        all_four = [both, swap(both, 1)]
        features = jnp.concatenate(
            [all_four[c][b][k] for k in range(group) for b in range(2) for c in range(2)],
            axis=-1,
        )
        found = [
            cross(jnp.dot(features[d], weights_in, preferred_element_type=f32).astype(bf16), d)
            for d in range(1, ndp)
        ]
        projected.append([jnp.dot(features[0], weights_in, preferred_element_type=f32)] + found)

    first_came = swap(after(first[1], both), 2)

    shared = after(shared, both)
    dt_raw = lax.dynamic_slice_in_dim(shared, 2 * STATE + me * heads, heads, 1)
    step_size = jax.nn.softplus(dt_raw + dt_bias)
    log_decay = -step_size * jnp.exp(a_log)
    causal = jnp.arange(length)[:, None] >= jnp.arange(length)[None, :]
    running = jnp.dot(causal.astype(f32), log_decay, precision=lax.Precision.HIGHEST)
    run_row, step_row = running.T, step_size.T
    scans = [scan_weights(n, rows, shared, running, run_row, step_row) for n in range(far)]
    skip = jnp.repeat(d_skip, SHEAD)[None, :]
    earlier, gated, gated_other, squares = [], [], [], []
    for n in range(far):
        pieces = []
        for m, size in enumerate(sizes):
            start, stop = ends[m] - size, ends[m]
            low, high = max(start, n * rows), min(stop, (n + 1) * rows)
            if low < high:
                pieces.append((projected[m], low - start, high - start))
        split, gated_n, squares_n = scan_chunk(
            n, rows, scans[n], pieces, earlier, skip, norm_gain[None, :]
        )
        earlier.append(split)
        gated.append(gated_n)
        gated_other.append(swap(gated_n, 1))
        squares.append(squares_n)
    weights = (gated, gated_other, mixer_out, mixer_there)
    gated[-1] = after(gated[-1], first_came)
    keep, send = project_out(0, width, (spots, far), *weights)
    squares = jnp.concatenate(squares)
    k = 1
    while k < nmp:
        if k == 4:
            squares = after(squares, send)
        squares = squares + swap(squares, k)
        k *= 2
    scale = lax.rsqrt(squares / (channels * nmp) + norm_eps).reshape(far, 2, rows // 2, 1)
    scale_kept = jnp.stack([at(at(scale, z ^ k), y) for k in range(far)])

    done, far_came = [], []
    for n in range(OUT_CHUNKS):
        if n == 0:
            keep, send = add_near(keep, swap(send, 2), scale_kept, first[0], first_came)
        else:
            keep, send = project_out(n * width, width, (spots, far), *weights, scale, *teacher)
            came = swap(send, 2)
            if n >= 2:
                came = after(came, far_came[n - 2])
            keep, send = add_near(keep, came)
        k = 1
        while k < far // 2:
            keep, send = add_near(keep, swap(send, 4 * k))
            k *= 2
        far_came.append(swap(send[0], 4 * k))
        done.append(keep[0])
    stay, came = finish(spots, done, far_came)
    came = swap(came, 1)
    return jnp.concatenate(
        [jnp.where(core == 0, stay, came), jnp.where(core == 0, came, stay)], axis=1
    )


def solution(mesh):
    placed = (
        P("dp", "mp"),
        P("dp", "mp"),
        P("dp", None),
        P("dp", None),
        P("mp", None),
        P(None, "dp", "mp"),
        P("mp", None),
        P("mp"),
        P("mp"),
        P("mp"),
        P("mp"),
        P("mp", None),
    )
    return jax.shard_map(
        functools.partial(local, mesh.shape["dp"], mesh.shape["mp"]),
        mesh=mesh,
        in_specs=placed,
        out_specs=P(("dp", "mp"), None),
        check_vma=False,
    )
```

```python
import functools

import jax
import jax.numpy as jnp
from jax import lax
from jax.experimental import pallas as pl
from jax.experimental.pallas import tpu as pltpu
from jax.sharding import PartitionSpec as P

HEAD = 128
SHEAD = 64
STATE = 128
LANES = 128
OUT_SPLIT = (1, 1, 1, 1)
SPLIT = (1, 1)
HINT = 16
OUT_TILE = 512
SMALL = 8 * 1024 * 1024
MIDDLE = 14 * 1024 * 1024
WIDE = 50 * 1024 * 1024
LARGE = 58 * 1024 * 1024

norm_eps = 1e-05
f32 = jnp.float32
bf16 = jnp.bfloat16


def cost(flops, moved):
    return pl.CostEstimate(flops=flops // HINT, bytes_accessed=moved // HINT, transcendentals=0)


def after(value, *events):
    return lax.optimization_barrier((value, *events))[0]


def pick(parts, index):
    chosen = parts[0]
    for m in range(1, len(parts)):
        chosen = jnp.where(index == m, parts[m], chosen)
    return chosen


def begin(hidden_in, shared_in, sizes):
    length, block = hidden_in.shape

    def body(hidden_ref, shared_ref, part_ref, *chunk_refs):
        at = 0
        for size, ref in zip(sizes, chunk_refs):
            ref[...] = hidden_ref[at : at + size]
            at += size
        part_ref[...] = jnp.dot(hidden_ref[...], shared_ref[...], preferred_element_type=f32)

    return pl.pallas_call(
        body,
        out_shape=(
            jax.ShapeDtypeStruct((length, shared_in.shape[1]), f32),
            *(jax.ShapeDtypeStruct((size, block), bf16) for size in sizes),
        ),
        compiler_params=pltpu.CompilerParams(vmem_limit_bytes=SMALL),
        cost_estimate=cost(2 * hidden_in.size * shared_in.shape[1], 4 * hidden_in.size),
        name="begin",
    )(hidden_in, shared_in)


def project_in(spot, features, weights):
    ndp = len(features[0])
    group, size, block = features[0][0].shape
    kinds, _, channels = weights.shape
    places = [(m, k) for m in range(len(features)) for k in range(group)]
    given = len(features) * ndp
    shape = (ndp * size, kinds * channels)

    def body(spot_ref, *refs):
        weights_ref = refs[given]
        tokens_ref, rows_ref, done = refs[-3:]
        copies = []
        for n, (m, k) in enumerate(places):
            row = pl.multiple_of((spot_ref[0] ^ (k * len(features) + m)) * block, block)
            for kind in range(kinds):
                copies.append(
                    pltpu.make_async_copy(
                        weights_ref.at[kind, pl.ds(row, block)],
                        rows_ref.at[kind, pl.ds(n * block, block)],
                        done.at[n * kinds + kind],
                    )
                )
        for copy in copies:
            copy.start()
        for n, (m, k) in enumerate(places):
            for d in range(ndp):
                tokens_ref[d * size : (d + 1) * size, n * block : (n + 1) * block] = refs[
                    m * ndp + d
                ][k]
        for copy in copies:
            copy.wait()
        for kind in range(kinds):
            lane = slice(kind * channels, (kind + 1) * channels)
            total = jnp.dot(tokens_ref[...], rows_ref[kind], preferred_element_type=f32)
            for d in range(ndp):
                out = refs[given + 1 + d]
                out[:, lane] = total[d * size : (d + 1) * size].astype(out.dtype)

    vmem = pl.BlockSpec(memory_space=pltpu.VMEM)
    outs = [
        jax.ShapeDtypeStruct((size, shape[1]), f32 if d == 0 else bf16) for d in range(ndp)
    ]
    deep = len(places) * block
    found = pl.pallas_call(
        body,
        in_specs=[pl.BlockSpec(memory_space=pltpu.SMEM)]
        + [vmem] * given
        + [pl.BlockSpec(memory_space=pltpu.HBM)],
        out_specs=[vmem] * len(outs),
        out_shape=outs,
        scratch_shapes=[
            pltpu.VMEM((ndp * size, deep), bf16),
            pltpu.VMEM((kinds, deep, channels), bf16),
            pltpu.SemaphoreType.DMA((len(places) * kinds,)),
        ],
        compiler_params=pltpu.CompilerParams(vmem_limit_bytes=WIDE),
        cost_estimate=cost(2 * deep * shape[0] * shape[1], 2 * deep * shape[1] + 6 * shape[0] * shape[1]),
        name="project_in",
    )(spot, *(a for way in features for a in way), weights)
    return list(found)


def attention(queries, key_rows, value_rows, kv_head):
    length, columns = queries.shape
    heads = columns // HEAD
    tall = min(length, 128)

    def body(kv_ref, q_ref, k_ref, v_ref, out_ref):
        for r in range(length // tall):
            seen = (r + 1) * tall
            at = slice(r * tall, seen)
            scores = lax.dot_general(
                q_ref[at], k_ref[:seen], (((1,), (1,)), ((), ())), preferred_element_type=f32
            ) * HEAD ** (-0.5)
            row = lax.broadcasted_iota(jnp.int32, (tall, seen), 0) + r * tall
            column = lax.broadcasted_iota(jnp.int32, (tall, seen), 1)
            scores = jnp.where(row >= column, scores, -jnp.inf)
            grown = jnp.exp(scores - jnp.max(scores, axis=1, keepdims=True))
            probs = (grown / jnp.sum(grown, axis=1, keepdims=True)).astype(bf16)
            out_ref[at] = jnp.dot(probs, v_ref[:seen], preferred_element_type=f32).astype(bf16)

    return pl.pallas_call(
        body,
        grid_spec=pltpu.PrefetchScalarGridSpec(
            num_scalar_prefetch=1,
            grid=(heads,),
            in_specs=[
                pl.BlockSpec((length, HEAD), lambda h, s: (0, h)),
                pl.BlockSpec((length, HEAD), lambda h, s: (0, s[0])),
                pl.BlockSpec((length, HEAD), lambda h, s: (0, s[0])),
            ],
            out_specs=pl.BlockSpec((length, HEAD), lambda h, s: (0, h)),
        ),
        out_shape=jax.ShapeDtypeStruct((length, columns), bf16),
        compiler_params=pltpu.CompilerParams(vmem_limit_bytes=SMALL),
        cost_estimate=cost(4 * length * length * columns, 4 * length * columns),
        name="attention",
    )(kv_head, queries, key_rows, value_rows)


def scan_weights(n, rows, shared, run_col, run_row, step_row):
    heads = run_row.shape[0]
    pairs = heads // 2
    wide = 2 * rows
    here = slice(n * rows, (n + 1) * rows)

    def body(shared_ref, col_ref, row_ref, step_ref, out_ref):
        below = lax.broadcasted_iota(jnp.int32, (rows, rows), 0) >= lax.broadcasted_iota(
            jnp.int32, (rows, rows), 1
        )
        for j in range(n + 1):
            there = slice(j * rows, (j + 1) * rows)
            contact = lax.dot_general(
                shared_ref[here, STATE : 2 * STATE],
                shared_ref[there, :STATE],
                (((1,), (1,)), ((), ())),
                precision=lax.Precision.HIGHEST,
                preferred_element_type=f32,
            )
            for h in range(heads):
                span = col_ref[here, h : h + 1] - row_ref[h : h + 1, there]
                if j == n:
                    span = jnp.where(below, span, -jnp.inf)
                weight = contact * jnp.exp(span) * step_ref[h : h + 1, there]
                high = weight.astype(bf16)
                low = (weight - high.astype(f32)).astype(bf16)
                at = (h % 2) * rows
                out_ref[h // 2, at : at + rows, j * wide : (j + 1) * wide] = jnp.concatenate(
                    [high, low], axis=1
                )

    grown = (n + 1) * rows
    return pl.pallas_call(
        body,
        out_shape=jax.ShapeDtypeStruct((pairs, wide, (n + 1) * wide), bf16),
        compiler_params=pltpu.CompilerParams(vmem_limit_bytes=SMALL),
        cost_estimate=cost(12 * grown * rows * STATE, 4 * heads * grown * rows),
        name="scan_weights",
    )(shared, run_col, run_row, step_row)


def scan_chunk(n, rows, weights, pieces, earlier, skip, gain):
    pairs, wide, _ = weights.shape
    channels = skip.shape[1]
    parts = [a for a, _, _ in pieces]
    count = 3 + sum(map(len, parts))

    def body(*refs):
        weights_ref, skip_ref, gain_ref = refs[:3]
        earlier_refs = refs[count : count + n]
        split_ref, gated_ref, squares_ref = refs[count + n :]

        def projected(lane):
            found, at = [], 3
            for arrays, start, stop in pieces:
                total = refs[at][start:stop, lane]
                for m in range(1, len(arrays)):
                    total = total + refs[at + m][start:stop, lane].astype(f32)
                at += len(arrays)
                found.append(total)
            return jnp.concatenate(found, axis=0) if len(found) > 1 else found[0]

        left = lax.broadcasted_iota(jnp.int32, (rows, LANES), 1) < SHEAD
        squares = jnp.zeros((rows, LANES), f32)
        for p in range(pairs):
            lane = slice(p * LANES, (p + 1) * LANES)
            gate_lane = slice(channels + p * LANES, channels + (p + 1) * LANES)
            x = projected(lane)
            gate = projected(gate_lane)
            high = x.astype(bf16)
            low = (x - high.astype(f32)).astype(bf16)
            both = jnp.concatenate([high, low], axis=1)
            split_ref[p] = jnp.concatenate([both, both], axis=0)
            total = jnp.dot(
                weights_ref[p, :, n * wide : (n + 1) * wide],
                split_ref[p],
                preferred_element_type=f32,
            )
            for j in range(n):
                total = total + jnp.dot(
                    weights_ref[p, :, j * wide : (j + 1) * wide],
                    earlier_refs[j][p],
                    preferred_element_type=f32,
                )
            total = total[:, :LANES] + total[:, LANES:]
            scanned = jnp.where(left, total[:rows], total[rows:])
            gated = (scanned + skip_ref[:, lane] * x) * (gate / (1.0 + jnp.exp(-gate)))
            squares = squares + gated * gated
            gated_ref[:, lane] = (gated * gain_ref[:, lane]).astype(bf16)
        squares_ref[...] = lax.dot_general(
            jnp.ones((8, LANES), f32),
            squares,
            (((1,), (1,)), ((), ())),
            precision=lax.Precision.HIGHEST,
            preferred_element_type=f32,
        )[:1]

    return pl.pallas_call(
        body,
        out_shape=(
            jax.ShapeDtypeStruct((pairs, wide, 2 * LANES), bf16),
            jax.ShapeDtypeStruct((rows, channels), bf16),
            jax.ShapeDtypeStruct((1, rows), f32),
        ),
        compiler_params=pltpu.CompilerParams(vmem_limit_bytes=MIDDLE),
        cost_estimate=cost(2 * pairs * wide * wide * 2 * LANES * (n + 1), 8 * rows * channels * 2),
        name="scan_chunk",
    )(weights, skip, gain, *(a for arrays in parts for a in arrays), *earlier)


def project_out(at, width, spots, here, there, weight, weight_there, scale=None, *teacher):
    spots, far = spots
    sets = [(here, there)] + ([teacher[:2]] if teacher else [])
    weights = [weight, weight_there] + list(teacher[2:])
    pieces = [p for pair in sets for group in pair for p in group]
    channels = here[0].shape[1]
    length = sum(p.shape[0] for p in here)
    half = weight_there.shape[1] // 2
    tile = min(OUT_TILE, width)
    steps = width // tile
    part = length // (2 * far)

    def body(spot_ref, *refs):
        weight_refs = refs[len(pieces) : len(pieces) + len(weights)]
        scale_ref = refs[len(pieces) + len(weights)]
        keep_ref, send_ref, rows_ref, tiles_ref, done = refs[-5:]
        z, y = spot_ref[0], spot_ref[1]
        own = pl.multiple_of(spot_ref[2] * half + at, LANES)
        copies = []
        for t in range(steps):
            for m, ref in enumerate(weight_refs):
                column = own + t * tile
                copies.append(
                    pltpu.make_async_copy(
                        ref.at[:, pl.ds(pl.multiple_of(column, LANES), tile)],
                        tiles_ref.at[t * len(weights) + m],
                        done.at[t * len(weights) + m],
                    )
                )
        for copy in copies:
            copy.start()
        from_row, slot = 0, 0
        for ref in refs[: len(pieces)]:
            size = ref.shape[0]
            rows_ref[slot, from_row : from_row + size] = ref[...]
            from_row += size
            if from_row == length:
                from_row, slot = 0, slot + 1
        for t in range(steps):
            lane = slice(t * tile, (t + 1) * tile)
            products = []
            for m in range(len(weights)):
                copies[t * len(weights) + m].wait()
            for m in range(0, len(weights), 2):
                first = t * len(weights) + m
                products.append(
                    jnp.dot(rows_ref[m], tiles_ref[first], preferred_element_type=f32)
                    + jnp.dot(rows_ref[m + 1], tiles_ref[first + 1], preferred_element_type=f32)
                )
            for zt in range(far):
                low = zt * 2 * part
                near, away = (
                    products[0][low + e * part : low + (e + 1) * part] for e in range(2)
                )
                if teacher:
                    near = near * scale_ref[zt, 0] - products[1][low : low + part]
                    away = away * scale_ref[zt, 1] - products[1][low + part : low + 2 * part]
                keep_ref[zt ^ z, :, lane] = jnp.where(y == 0, near, away)
                send_ref[zt ^ z, :, lane] = jnp.where(y == 0, away, near).astype(bf16)

    return pl.pallas_call(
        body,
        in_specs=[pl.BlockSpec(memory_space=pltpu.SMEM)]
        + [pl.BlockSpec(memory_space=pltpu.VMEM)] * len(pieces)
        + [pl.BlockSpec(memory_space=pltpu.HBM)] * len(weights)
        + ([pl.BlockSpec(memory_space=pltpu.VMEM)] if teacher else []),
        out_specs=[pl.BlockSpec(memory_space=pltpu.VMEM)] * 2,
        out_shape=(
            jax.ShapeDtypeStruct((far, part, width), f32),
            jax.ShapeDtypeStruct((far, part, width), bf16),
        ),
        scratch_shapes=[
            pltpu.VMEM((len(weights), length, channels), bf16),
            pltpu.VMEM((steps * len(weights), channels, tile), bf16),
            pltpu.SemaphoreType.DMA((steps * len(weights),)),
        ],
        compiler_params=pltpu.CompilerParams(vmem_limit_bytes=LARGE if teacher else WIDE),
        cost_estimate=cost(
            2 * len(weights) * length * channels * width,
            2 * len(weights) * channels * width + 6 * length * width,
        ),
        name="project_out",
    )(spots, *pieces, *weights, *([scale] if teacher else []))


def add_near(keep, came, scale=None, teacher=None, teacher_came=None):
    far, part, width = keep.shape
    stay = far // 2
    extra = [a for a in (scale, teacher, teacher_came) if a is not None]

    def body(keep_ref, came_ref, *refs):
        stay_ref, send_ref = refs[-2:]
        for k in range(far):
            total = keep_ref[k] + came_ref[k].astype(f32)
            if extra:
                total = total * refs[0][k] - (refs[1][k] + refs[2][k].astype(f32))
            if k % 2 == 0:
                stay_ref[k // 2] = total
            else:
                send_ref[k // 2] = total.astype(bf16)

    return pl.pallas_call(
        body,
        out_shape=(
            jax.ShapeDtypeStruct((stay, part, width), f32),
            jax.ShapeDtypeStruct((stay, part, width), bf16),
        ),
        compiler_params=pltpu.CompilerParams(vmem_limit_bytes=SMALL),
        cost_estimate=cost(keep.size, 8 * keep.size),
        name="add_near",
    )(keep, came, *extra)


def finish(spots, kept, came):
    rows = kept[0].shape[0] // 2
    count = len(kept)
    starts = [sum(a.shape[1] for a in kept[:n]) for n in range(count + 1)]
    width = starts[count]

    def body(spot_ref, *refs):
        own_ref, other_ref = refs[-2:]
        core = spot_ref[2]
        for n in range(count):
            total = (refs[n][...] + refs[count + n][...].astype(f32)).astype(bf16)
            low, high = total[:rows], total[rows:]
            lane = slice(starts[n], starts[n + 1])
            own_ref[:, lane] = jnp.where(core == 0, low, high)
            other_ref[:, lane] = jnp.where(core == 0, high, low)

    return pl.pallas_call(
        body,
        in_specs=[pl.BlockSpec(memory_space=pltpu.SMEM)]
        + [pl.BlockSpec(memory_space=pltpu.VMEM)] * (2 * count),
        out_shape=(jax.ShapeDtypeStruct((rows, width), bf16),) * 2,
        compiler_params=pltpu.CompilerParams(vmem_limit_bytes=SMALL),
        cost_estimate=cost(rows * 2 * width, 16 * rows * width),
        name="finish",
    )(spots, *kept, *came)


def local(
    ndp,
    nmp,
    hidden_in,
    queries,
    key_rows,
    value_rows,
    teacher_proj,
    mixer_in,
    shared_in,
    dt_bias,
    a_log,
    d_skip,
    norm_gain,
    mixer_out,
):
    far = nmp // 4
    group = far // ndp
    me = lax.axis_index("mp")
    seq = lax.axis_index("dp")
    core, y, z = me % 2, (me // 2) % 2, me // 4

    def swap(source, k):
        return lax.ppermute(source, "mp", [(s, s ^ k) for s in range(nmp)])

    def cross(source, k):
        return lax.ppermute(source, "dp", [(s, s ^ k) for s in range(ndp)])

    length, block = hidden_in.shape
    channels = mixer_in.shape[2]
    heads = dt_bias.shape[0]
    rows = length // far
    spots = jnp.stack([z, y, core]).astype(jnp.int32)

    def at(source, index):
        return lax.dynamic_index_in_dim(source, index, 0, False)

    sizes = [length * share // sum(SPLIT) for share in SPLIT]
    ends = [sum(sizes[: n + 1]) for n in range(len(sizes))]
    shared, *chunks = begin(hidden_in, shared_in, sizes)
    half = mixer_out.shape[1] // 2
    widths = [half * share // sum(OUT_SPLIT) for share in OUT_SPLIT]
    head_count = queries.shape[1] // HEAD
    kv_heads = key_rows.shape[1] // HEAD
    kv_head = (me * head_count // (head_count * nmp // kv_heads)).astype(jnp.int32).reshape(1)
    turn = (z // group) ^ seq
    spot = (me % (4 * group)).astype(jnp.int32).reshape(1)
    distances = [0]
    k = far // 2
    while k:
        distances += [d + k for d in distances]
        k //= 2
    order = [distances.index(d) for d in range(far)]
    before = {}

    def in_turn(step, value):
        return after(value, before[step]) if step in before else value

    def fold(value, k, bit):
        value = value.reshape(2, value.shape[0] // 2, -1)
        return at(value, bit) + swap(at(value, 1 - bit), k)

    def unfold(value, k, bit):
        came = swap(value, k)
        return jnp.concatenate([jnp.where(bit == 0, value, came), jnp.where(bit == 0, came, value)])

    shared = fold(shared, 1, core)
    teacher_there, mixer_there = (
        swap(after(weight, shared), 1) for weight in (teacher_proj, mixer_out)
    )
    bits = [1 << e for e in range(far.bit_length() - 1)]
    context = attention(queries, key_rows, value_rows, kv_head)
    teacher = ([context], [swap(context, 1)], teacher_proj, teacher_there)
    projected, aways, squares_in = [], [], []
    last = len(sizes) - 1
    for n, size in enumerate(sizes):
        line = [chunks[n]]
        k = far // 2
        while k:
            packed = in_turn(k, jnp.stack(line))
            if n == 0 and k == 1:
                packed = after(packed, context)
            near = before[k] = swap(packed, 4 * k)
            if k == far // 2:
                front = near
            line = line + [near[m] for m in range(len(line))]
            k //= 2
        line = [line[m] for m in order]
        line = [jnp.stack(line[m * group : (m + 1) * group]) for m in range(ndp)]
        square = [pick(line, turn ^ d) for d in range(ndp)]
        away = in_turn("dp", tuple(square[1:]))
        if n == 1:
            away = after(away, teacher_there, mixer_there)
        if n == 0:
            shared = fold(after(shared, front), 2, y)
        square = [square[0]] + [cross(away[d - 1], d) for d in range(1, ndp)]
        before["dp"] = square[1:]
        if n == 1:
            shared = after(shared, front)
            for k in reversed(bits[1:]):
                shared = fold(shared, 4 * k, (z // k) % 2)
            shared = unfold(fold(after(shared, near), 4, z % 2), 4, z % 2)
            for k in bits[1:]:
                shared = unfold(shared, 4 * k, (z // k) % 2)
        aways.append(away)
        squares_in.append(square)
    for n, square in enumerate(squares_in):
        came = []
        for d in range(ndp):
            sent = in_turn(("y", d), square[d])
            if n == last and d == 0:
                first = project_out(0, widths[0], (spots, far), *teacher)
            if n == last and d == 1:
                sent = after(sent, *found)
            came.append(swap(sent, 2))
            before["y", d] = came[d]
        if n == last:
            shared = unfold(unfold(after(shared, came[0]), 2, y), 1, core)
        if n < last:
            came = list(after(tuple(came), *aways[n + 1]))
        ways = square, [swap(after(a, came[0]), 1) for a in square], came, [swap(a, 1) for a in came]
        found = project_in(spot, ways, mixer_in)
        projected.append([found[0]] + [cross(found[d], d) for d in range(1, ndp)])
    first_came = swap(after(first[1], came), 2)

    dt_raw = lax.dynamic_slice_in_dim(shared, 2 * STATE + me * heads, heads, 1)
    step_size = jax.nn.softplus(dt_raw + dt_bias)
    log_decay = -step_size * jnp.exp(a_log)
    causal = jnp.arange(length)[:, None] >= jnp.arange(length)[None, :]
    running = jnp.dot(causal.astype(f32), log_decay, precision=lax.Precision.HIGHEST)
    run_row, step_row = running.T, step_size.T
    scans = [scan_weights(n, rows, shared, running, run_row, step_row) for n in range(far)]
    skip = jnp.repeat(d_skip, SHEAD)[None, :]
    earlier, gated, gated_other, squares = [], [], [], []
    for n in range(far):
        pieces = []
        for m, size in enumerate(sizes):
            start, stop = ends[m] - size, ends[m]
            low, high = max(start, n * rows), min(stop, (n + 1) * rows)
            if low < high:
                pieces.append((projected[m], low - start, high - start))
        split, gated_n, squares_n = scan_chunk(
            n, rows, scans[n], pieces, earlier, skip, norm_gain[None, :]
        )
        earlier.append(split)
        gated.append(gated_n)
        gated_other.append(swap(gated_n, 1))
        squares.append(squares_n)
    weights = (gated, gated_other, mixer_out, mixer_there)
    gated[-1] = after(gated[-1], first_came)
    keep, send = project_out(0, widths[0], (spots, far), *weights)
    squares = jnp.concatenate(squares)
    k = 1
    while k < nmp:
        if k == 4:
            squares = after(squares, send)
        squares = squares + swap(squares, k)
        k *= 2
    scale = lax.rsqrt(squares / (channels * nmp) + norm_eps).reshape(far, 2, rows // 2, 1)
    scale_kept = jnp.stack([at(at(scale, z ^ k), y) for k in range(far)])

    done, far_came = [], []
    for n, width in enumerate(widths):
        if n == 0:
            keep, send = add_near(keep, swap(send, 2), scale_kept, first[0], first_came)
        else:
            keep, send = project_out(
                sum(widths[:n]), width, (spots, far), *weights, scale, *teacher
            )
            came = swap(send, 2)
            if n >= 2:
                came = after(came, far_came[n - 2])
            keep, send = add_near(keep, came)
        k = 1
        while k < far // 2:
            keep, send = add_near(keep, swap(send, 4 * k))
            k *= 2
        far_came.append(swap(send[0], 4 * k))
        done.append(keep[0])
    stay, came = finish(spots, done, far_came)
    came = swap(came, 1)
    return jnp.concatenate(
        [jnp.where(core == 0, stay, came), jnp.where(core == 0, came, stay)], axis=1
    )


def solution(mesh):
    placed = (
        P("dp", "mp"),
        P("dp", "mp"),
        P("dp", None),
        P("dp", None),
        P("mp", None),
        P(None, "dp", "mp"),
        P("mp", None),
        P("mp"),
        P("mp"),
        P("mp"),
        P("mp"),
        P("mp", None),
    )
    return jax.shard_map(
        functools.partial(local, mesh.shape["dp"], mesh.shape["mp"]),
        mesh=mesh,
        in_specs=placed,
        out_specs=P(("dp", "mp"), None),
        check_vma=False,
    )
```

```python
import functools

import jax
import jax.numpy as jnp
from jax import lax
from jax.experimental import pallas as pl
from jax.experimental.pallas import tpu as pltpu
from jax.sharding import PartitionSpec as P

HEAD = 128
SHEAD = 64
STATE = 128
LANES = 128
OUT_SPLIT = (1, 1, 1, 1)
SPLIT = (1, 1)
HINT = 16
OUT_TILE = 512
SMALL = 8 * 1024 * 1024
MIDDLE = 14 * 1024 * 1024
WIDE = 50 * 1024 * 1024
LARGE = 58 * 1024 * 1024

norm_eps = 1e-05
f32 = jnp.float32
bf16 = jnp.bfloat16


def cost(flops, moved):
    return pl.CostEstimate(flops=flops // HINT, bytes_accessed=moved // HINT, transcendentals=0)


def after(value, *events):
    return lax.optimization_barrier((value, *events))[0]


def pick(parts, index):
    chosen = parts[0]
    for m in range(1, len(parts)):
        chosen = jnp.where(index == m, parts[m], chosen)
    return chosen


def begin(hidden_in, shared_in, sizes):
    length, block = hidden_in.shape

    def body(hidden_ref, shared_ref, part_ref, *chunk_refs):
        at = 0
        for size, ref in zip(sizes, chunk_refs):
            ref[...] = hidden_ref[at : at + size]
            at += size
        part_ref[...] = jnp.dot(hidden_ref[...], shared_ref[...], preferred_element_type=f32)

    return pl.pallas_call(
        body,
        out_shape=(
            jax.ShapeDtypeStruct((length, shared_in.shape[1]), f32),
            *(jax.ShapeDtypeStruct((size, block), bf16) for size in sizes),
        ),
        compiler_params=pltpu.CompilerParams(vmem_limit_bytes=SMALL),
        cost_estimate=cost(2 * hidden_in.size * shared_in.shape[1], 4 * hidden_in.size),
        name="begin",
    )(hidden_in, shared_in)


def project_in(spot, features, weights):
    ndp = len(features[0])
    group, size, block = features[0][0].shape
    kinds, _, channels = weights.shape
    places = [(m, k) for m in range(len(features)) for k in range(group)]
    given = len(features) * ndp
    shape = (ndp * size, kinds * channels)

    def body(spot_ref, *refs):
        weights_ref = refs[given]
        tokens_ref, rows_ref, done = refs[-3:]
        copies = []
        for kind in range(kinds):
            for n, (m, k) in enumerate(places):
                row = pl.multiple_of((spot_ref[0] ^ (k * len(features) + m)) * block, block)
                copies.append(
                    pltpu.make_async_copy(
                        weights_ref.at[kind, pl.ds(row, block)],
                        rows_ref.at[kind, pl.ds(n * block, block)],
                        done.at[kind * len(places) + n],
                    )
                )
        for copy in copies:
            copy.start()
        for n, (m, k) in enumerate(places):
            for d in range(ndp):
                tokens_ref[d * size : (d + 1) * size, n * block : (n + 1) * block] = refs[
                    m * ndp + d
                ][k]
        for kind in range(kinds):
            for copy in copies[kind * len(places) : (kind + 1) * len(places)]:
                copy.wait()
            lane = slice(kind * channels, (kind + 1) * channels)
            total = jnp.dot(tokens_ref[...], rows_ref[kind], preferred_element_type=f32)
            for d in range(ndp):
                out = refs[given + 1 + d]
                out[:, lane] = total[d * size : (d + 1) * size].astype(out.dtype)

    vmem = pl.BlockSpec(memory_space=pltpu.VMEM)
    outs = [
        jax.ShapeDtypeStruct((size, shape[1]), f32 if d == 0 else bf16) for d in range(ndp)
    ]
    deep = len(places) * block
    found = pl.pallas_call(
        body,
        in_specs=[pl.BlockSpec(memory_space=pltpu.SMEM)]
        + [vmem] * given
        + [pl.BlockSpec(memory_space=pltpu.HBM)],
        out_specs=[vmem] * len(outs),
        out_shape=outs,
        scratch_shapes=[
            pltpu.VMEM((ndp * size, deep), bf16),
            pltpu.VMEM((kinds, deep, channels), bf16),
            pltpu.SemaphoreType.DMA((len(places) * kinds,)),
        ],
        compiler_params=pltpu.CompilerParams(vmem_limit_bytes=WIDE),
        cost_estimate=cost(2 * deep * shape[0] * shape[1], 2 * deep * shape[1] + 6 * shape[0] * shape[1]),
        name="project_in",
    )(spot, *(a for way in features for a in way), weights)
    return list(found)


def attention(queries, key_rows, value_rows, kv_head):
    length, columns = queries.shape
    heads = columns // HEAD
    tall = min(length, 128)

    def body(kv_ref, q_ref, k_ref, v_ref, out_ref):
        for r in range(length // tall):
            seen = (r + 1) * tall
            at = slice(r * tall, seen)
            scores = lax.dot_general(
                q_ref[at], k_ref[:seen], (((1,), (1,)), ((), ())), preferred_element_type=f32
            ) * HEAD ** (-0.5)
            row = lax.broadcasted_iota(jnp.int32, (tall, seen), 0) + r * tall
            column = lax.broadcasted_iota(jnp.int32, (tall, seen), 1)
            scores = jnp.where(row >= column, scores, -jnp.inf)
            grown = jnp.exp(scores - jnp.max(scores, axis=1, keepdims=True))
            probs = (grown / jnp.sum(grown, axis=1, keepdims=True)).astype(bf16)
            out_ref[at] = jnp.dot(probs, v_ref[:seen], preferred_element_type=f32).astype(bf16)

    return pl.pallas_call(
        body,
        grid_spec=pltpu.PrefetchScalarGridSpec(
            num_scalar_prefetch=1,
            grid=(heads,),
            in_specs=[
                pl.BlockSpec((length, HEAD), lambda h, s: (0, h)),
                pl.BlockSpec((length, HEAD), lambda h, s: (0, s[0])),
                pl.BlockSpec((length, HEAD), lambda h, s: (0, s[0])),
            ],
            out_specs=pl.BlockSpec((length, HEAD), lambda h, s: (0, h)),
        ),
        out_shape=jax.ShapeDtypeStruct((length, columns), bf16),
        compiler_params=pltpu.CompilerParams(vmem_limit_bytes=SMALL),
        cost_estimate=cost(4 * length * length * columns, 4 * length * columns),
        name="attention",
    )(kv_head, queries, key_rows, value_rows)


def scan_weights(n, rows, shared, run_col, run_row, step_row):
    heads = run_row.shape[0]
    pairs = heads // 2
    wide = 2 * rows
    here = slice(n * rows, (n + 1) * rows)

    def body(shared_ref, col_ref, row_ref, step_ref, out_ref):
        below = lax.broadcasted_iota(jnp.int32, (rows, rows), 0) >= lax.broadcasted_iota(
            jnp.int32, (rows, rows), 1
        )
        for j in range(n + 1):
            there = slice(j * rows, (j + 1) * rows)
            contact = lax.dot_general(
                shared_ref[here, STATE : 2 * STATE],
                shared_ref[there, :STATE],
                (((1,), (1,)), ((), ())),
                precision=lax.Precision.HIGHEST,
                preferred_element_type=f32,
            )
            for h in range(heads):
                span = col_ref[here, h : h + 1] - row_ref[h : h + 1, there]
                if j == n:
                    span = jnp.where(below, span, -jnp.inf)
                weight = contact * jnp.exp(span) * step_ref[h : h + 1, there]
                high = weight.astype(bf16)
                low = (weight - high.astype(f32)).astype(bf16)
                at = (h % 2) * rows
                out_ref[h // 2, at : at + rows, j * wide : (j + 1) * wide] = jnp.concatenate(
                    [high, low], axis=1
                )

    grown = (n + 1) * rows
    return pl.pallas_call(
        body,
        out_shape=jax.ShapeDtypeStruct((pairs, wide, (n + 1) * wide), bf16),
        compiler_params=pltpu.CompilerParams(vmem_limit_bytes=SMALL),
        cost_estimate=cost(12 * grown * rows * STATE, 4 * heads * grown * rows),
        name="scan_weights",
    )(shared, run_col, run_row, step_row)


def scan_chunk(n, rows, weights, pieces, earlier, skip, gain):
    pairs, wide, _ = weights.shape
    channels = skip.shape[1]
    parts = [a for a, _, _ in pieces]
    count = 3 + sum(map(len, parts))

    def body(*refs):
        weights_ref, skip_ref, gain_ref = refs[:3]
        earlier_refs = refs[count : count + n]
        split_ref, gated_ref, squares_ref = refs[count + n :]

        def projected(lane):
            found, at = [], 3
            for arrays, start, stop in pieces:
                total = refs[at][start:stop, lane]
                for m in range(1, len(arrays)):
                    total = total + refs[at + m][start:stop, lane].astype(f32)
                at += len(arrays)
                found.append(total)
            return jnp.concatenate(found, axis=0) if len(found) > 1 else found[0]

        left = lax.broadcasted_iota(jnp.int32, (rows, LANES), 1) < SHEAD
        squares = jnp.zeros((rows, LANES), f32)
        for p in range(pairs):
            lane = slice(p * LANES, (p + 1) * LANES)
            gate_lane = slice(channels + p * LANES, channels + (p + 1) * LANES)
            x = projected(lane)
            gate = projected(gate_lane)
            high = x.astype(bf16)
            low = (x - high.astype(f32)).astype(bf16)
            both = jnp.concatenate([high, low], axis=1)
            split_ref[p] = jnp.concatenate([both, both], axis=0)
            total = jnp.dot(
                weights_ref[p, :, n * wide : (n + 1) * wide],
                split_ref[p],
                preferred_element_type=f32,
            )
            for j in range(n):
                total = total + jnp.dot(
                    weights_ref[p, :, j * wide : (j + 1) * wide],
                    earlier_refs[j][p],
                    preferred_element_type=f32,
                )
            total = total[:, :LANES] + total[:, LANES:]
            scanned = jnp.where(left, total[:rows], total[rows:])
            gated = (scanned + skip_ref[:, lane] * x) * (gate / (1.0 + jnp.exp(-gate)))
            squares = squares + gated * gated
            gated_ref[:, lane] = (gated * gain_ref[:, lane]).astype(bf16)
        squares_ref[...] = lax.dot_general(
            jnp.ones((8, LANES), f32),
            squares,
            (((1,), (1,)), ((), ())),
            precision=lax.Precision.HIGHEST,
            preferred_element_type=f32,
        )[:1]

    return pl.pallas_call(
        body,
        out_shape=(
            jax.ShapeDtypeStruct((pairs, wide, 2 * LANES), bf16),
            jax.ShapeDtypeStruct((rows, channels), bf16),
            jax.ShapeDtypeStruct((1, rows), f32),
        ),
        compiler_params=pltpu.CompilerParams(vmem_limit_bytes=MIDDLE),
        cost_estimate=cost(2 * pairs * wide * wide * 2 * LANES * (n + 1), 8 * rows * channels * 2),
        name="scan_chunk",
    )(weights, skip, gain, *(a for arrays in parts for a in arrays), *earlier)


def project_out(at, width, spots, here, there, weight, weight_there, scale=None, *teacher):
    spots, far = spots
    sets = [(here, there)] + ([teacher[:2]] if teacher else [])
    weights = [weight, weight_there] + list(teacher[2:])
    pieces = [p for pair in sets for group in pair for p in group]
    channels = here[0].shape[1]
    length = sum(p.shape[0] for p in here)
    half = weight_there.shape[1] // 2
    tile = min(OUT_TILE, width)
    steps = width // tile
    part = length // (2 * far)

    def body(spot_ref, *refs):
        weight_refs = refs[len(pieces) : len(pieces) + len(weights)]
        scale_ref = refs[len(pieces) + len(weights)]
        keep_ref, send_ref, rows_ref, tiles_ref, done = refs[-5:]
        z, y = spot_ref[0], spot_ref[1]
        own = pl.multiple_of(spot_ref[2] * half + at, LANES)
        copies = []
        for t in range(steps):
            for m, ref in enumerate(weight_refs):
                column = own + t * tile
                copies.append(
                    pltpu.make_async_copy(
                        ref.at[:, pl.ds(pl.multiple_of(column, LANES), tile)],
                        tiles_ref.at[t * len(weights) + m],
                        done.at[t * len(weights) + m],
                    )
                )
        for copy in copies:
            copy.start()
        from_row, slot = 0, 0
        for ref in refs[: len(pieces)]:
            size = ref.shape[0]
            rows_ref[slot, from_row : from_row + size] = ref[...]
            from_row += size
            if from_row == length:
                from_row, slot = 0, slot + 1
        for t in range(steps):
            lane = slice(t * tile, (t + 1) * tile)
            products = []
            for m in range(len(weights)):
                copies[t * len(weights) + m].wait()
            for m in range(0, len(weights), 2):
                first = t * len(weights) + m
                products.append(
                    jnp.dot(rows_ref[m], tiles_ref[first], preferred_element_type=f32)
                    + jnp.dot(rows_ref[m + 1], tiles_ref[first + 1], preferred_element_type=f32)
                )
            for zt in range(far):
                low = zt * 2 * part
                near, away = (
                    products[0][low + e * part : low + (e + 1) * part] for e in range(2)
                )
                if teacher:
                    near = near * scale_ref[zt, 0] - products[1][low : low + part]
                    away = away * scale_ref[zt, 1] - products[1][low + part : low + 2 * part]
                keep_ref[zt ^ z, :, lane] = jnp.where(y == 0, near, away)
                send_ref[zt ^ z, :, lane] = jnp.where(y == 0, away, near).astype(bf16)

    return pl.pallas_call(
        body,
        in_specs=[pl.BlockSpec(memory_space=pltpu.SMEM)]
        + [pl.BlockSpec(memory_space=pltpu.VMEM)] * len(pieces)
        + [pl.BlockSpec(memory_space=pltpu.HBM)] * len(weights)
        + ([pl.BlockSpec(memory_space=pltpu.VMEM)] if teacher else []),
        out_specs=[pl.BlockSpec(memory_space=pltpu.VMEM)] * 2,
        out_shape=(
            jax.ShapeDtypeStruct((far, part, width), f32),
            jax.ShapeDtypeStruct((far, part, width), bf16),
        ),
        scratch_shapes=[
            pltpu.VMEM((len(weights), length, channels), bf16),
            pltpu.VMEM((steps * len(weights), channels, tile), bf16),
            pltpu.SemaphoreType.DMA((steps * len(weights),)),
        ],
        compiler_params=pltpu.CompilerParams(vmem_limit_bytes=LARGE if teacher else WIDE),
        cost_estimate=cost(
            2 * len(weights) * length * channels * width,
            2 * len(weights) * channels * width + 6 * length * width,
        ),
        name="project_out",
    )(spots, *pieces, *weights, *([scale] if teacher else []))


def add_near(keep, came, scale=None, teacher=None, teacher_came=None):
    far, part, width = keep.shape
    stay = far // 2
    extra = [a for a in (scale, teacher, teacher_came) if a is not None]

    def body(keep_ref, came_ref, *refs):
        stay_ref, send_ref = refs[-2:]
        for k in range(far):
            total = keep_ref[k] + came_ref[k].astype(f32)
            if extra:
                total = total * refs[0][k] - (refs[1][k] + refs[2][k].astype(f32))
            if k % 2 == 0:
                stay_ref[k // 2] = total
            else:
                send_ref[k // 2] = total.astype(bf16)

    return pl.pallas_call(
        body,
        out_shape=(
            jax.ShapeDtypeStruct((stay, part, width), f32),
            jax.ShapeDtypeStruct((stay, part, width), bf16),
        ),
        compiler_params=pltpu.CompilerParams(vmem_limit_bytes=SMALL),
        cost_estimate=cost(keep.size, 8 * keep.size),
        name="add_near",
    )(keep, came, *extra)


def finish(spots, kept, came):
    rows = kept[0].shape[0] // 2
    count = len(kept)
    starts = [sum(a.shape[1] for a in kept[:n]) for n in range(count + 1)]
    width = starts[count]

    def body(spot_ref, *refs):
        own_ref, other_ref = refs[-2:]
        core = spot_ref[2]
        for n in range(count):
            total = (refs[n][...] + refs[count + n][...].astype(f32)).astype(bf16)
            low, high = total[:rows], total[rows:]
            lane = slice(starts[n], starts[n + 1])
            own_ref[:, lane] = jnp.where(core == 0, low, high)
            other_ref[:, lane] = jnp.where(core == 0, high, low)

    return pl.pallas_call(
        body,
        in_specs=[pl.BlockSpec(memory_space=pltpu.SMEM)]
        + [pl.BlockSpec(memory_space=pltpu.VMEM)] * (2 * count),
        out_shape=(jax.ShapeDtypeStruct((rows, width), bf16),) * 2,
        compiler_params=pltpu.CompilerParams(vmem_limit_bytes=SMALL),
        cost_estimate=cost(rows * 2 * width, 16 * rows * width),
        name="finish",
    )(spots, *kept, *came)


def local(
    ndp,
    nmp,
    hidden_in,
    queries,
    key_rows,
    value_rows,
    teacher_proj,
    mixer_in,
    shared_in,
    dt_bias,
    a_log,
    d_skip,
    norm_gain,
    mixer_out,
):
    far = nmp // 4
    group = far // ndp
    me = lax.axis_index("mp")
    seq = lax.axis_index("dp")
    core, y, z = me % 2, (me // 2) % 2, me // 4

    def swap(source, k):
        return lax.ppermute(source, "mp", [(s, s ^ k) for s in range(nmp)])

    def cross(source, k):
        return lax.ppermute(source, "dp", [(s, s ^ k) for s in range(ndp)])

    length, block = hidden_in.shape
    channels = mixer_in.shape[2]
    heads = dt_bias.shape[0]
    rows = length // far
    spots = jnp.stack([z, y, core]).astype(jnp.int32)

    def at(source, index):
        return lax.dynamic_index_in_dim(source, index, 0, False)

    sizes = [length * share // sum(SPLIT) for share in SPLIT]
    ends = [sum(sizes[: n + 1]) for n in range(len(sizes))]
    shared, *chunks = begin(hidden_in, shared_in, sizes)
    half = mixer_out.shape[1] // 2
    widths = [half * share // sum(OUT_SPLIT) for share in OUT_SPLIT]
    head_count = queries.shape[1] // HEAD
    kv_heads = key_rows.shape[1] // HEAD
    kv_head = (me * head_count // (head_count * nmp // kv_heads)).astype(jnp.int32).reshape(1)
    turn = (z // group) ^ seq
    spot = (me % (4 * group)).astype(jnp.int32).reshape(1)
    distances = [0]
    k = far // 2
    while k:
        distances += [d + k for d in distances]
        k //= 2
    order = [distances.index(d) for d in range(far)]
    before = {}

    def in_turn(step, value):
        return after(value, before[step]) if step in before else value

    def fold(value, k, bit):
        value = value.reshape(2, value.shape[0] // 2, -1)
        return at(value, bit) + swap(at(value, 1 - bit), k)

    def unfold(value, k, bit):
        came = swap(value, k)
        return jnp.concatenate([jnp.where(bit == 0, value, came), jnp.where(bit == 0, came, value)])

    shared = fold(shared, 1, core)
    teacher_there, mixer_there = (
        swap(after(weight, shared), 1) for weight in (teacher_proj, mixer_out)
    )
    bits = [1 << e for e in range(far.bit_length() - 1)]
    context = attention(queries, key_rows, value_rows, kv_head)
    teacher = ([context], [swap(context, 1)], teacher_proj, teacher_there)
    projected, aways, squares_in = [], [], []
    last = len(sizes) - 1
    for n, size in enumerate(sizes):
        line = [chunks[n]]
        k = far // 2
        while k:
            packed = in_turn(k, jnp.stack(line))
            if n == 0 and k == 1:
                packed = after(packed, context)
            near = before[k] = swap(packed, 4 * k)
            if k == far // 2:
                front = near
            line = line + [near[m] for m in range(len(line))]
            k //= 2
        line = [line[m] for m in order]
        line = [jnp.stack(line[m * group : (m + 1) * group]) for m in range(ndp)]
        square = [pick(line, turn ^ d) for d in range(ndp)]
        away = in_turn("dp", tuple(square[1:]))
        if n == 1:
            away = after(away, teacher_there, mixer_there)
        if n == 0:
            shared = fold(after(shared, front), 2, y)
        square = [square[0]] + [cross(away[d - 1], d) for d in range(1, ndp)]
        before["dp"] = square[1:]
        if n == 1:
            shared = after(shared, front)
            for k in reversed(bits[1:]):
                shared = fold(shared, 4 * k, (z // k) % 2)
            shared = unfold(fold(after(shared, near), 4, z % 2), 4, z % 2)
            for k in bits[1:]:
                shared = unfold(shared, 4 * k, (z // k) % 2)
        aways.append(away)
        squares_in.append(square)
    for n, square in enumerate(squares_in):
        came = []
        for d in range(ndp):
            sent = in_turn(("y", d), square[d])
            if n == last and d == 0:
                first = project_out(0, widths[0], (spots, far), *teacher)
            if n == last and d == 1:
                sent = after(sent, *found)
            came.append(swap(sent, 2))
            before["y", d] = came[d]
        if n == last:
            shared = unfold(unfold(after(shared, came[0]), 2, y), 1, core)
        if n < last:
            came = list(after(tuple(came), *aways[n + 1]))
        ways = square, [swap(after(a, came[0]), 1) for a in square], came, [swap(a, 1) for a in came]
        found = project_in(spot, ways, mixer_in)
        projected.append([found[0]] + [cross(found[d], d) for d in range(1, ndp)])
    first_came = swap(after(first[1], came), 2)

    dt_raw = lax.dynamic_slice_in_dim(shared, 2 * STATE + me * heads, heads, 1)
    step_size = jax.nn.softplus(dt_raw + dt_bias)
    log_decay = -step_size * jnp.exp(a_log)
    causal = jnp.arange(length)[:, None] >= jnp.arange(length)[None, :]
    running = jnp.dot(causal.astype(f32), log_decay, precision=lax.Precision.HIGHEST)
    run_row, step_row = running.T, step_size.T
    scans = [scan_weights(n, rows, shared, running, run_row, step_row) for n in range(far)]
    skip = jnp.repeat(d_skip, SHEAD)[None, :]
    earlier, gated, gated_other, squares = [], [], [], []
    for n in range(far):
        pieces = []
        for m, size in enumerate(sizes):
            start, stop = ends[m] - size, ends[m]
            low, high = max(start, n * rows), min(stop, (n + 1) * rows)
            if low < high:
                pieces.append((projected[m], low - start, high - start))
        split, gated_n, squares_n = scan_chunk(
            n, rows, scans[n], pieces, earlier, skip, norm_gain[None, :]
        )
        earlier.append(split)
        gated.append(gated_n)
        gated_other.append(swap(gated_n, 1))
        squares.append(squares_n)
    weights = (gated, gated_other, mixer_out, mixer_there)
    gated[-1] = after(gated[-1], first_came)
    keep, send = project_out(0, widths[0], (spots, far), *weights)
    squares = jnp.concatenate(squares)
    for k in (1, 2):
        squares = squares + swap(squares, k)
    squares = after(squares, send)
    squares = sum((swap(squares, 4 * k) for k in range(1, far)), squares)
    scale = lax.rsqrt(squares / (channels * nmp) + norm_eps).reshape(far, 2, rows // 2, 1)
    scale_kept = jnp.stack([at(at(scale, z ^ k), y) for k in range(far)])

    done, near_done, far_came = [], [], []
    for n, width in enumerate(widths):
        if n == 0:
            keep, send = add_near(keep, swap(send, 2), scale_kept, first[0], first_came)
        else:
            keep, send = project_out(
                sum(widths[:n]), width, (spots, far), *weights, scale, *teacher
            )
            came = swap(send, 2)
            if n >= 2:
                came = after(came, near_done[n - 2], *far_came[: n - 2])
            keep, send = add_near(keep, came)
        k = 1
        while k < far // 2:
            keep, send = add_near(keep, swap(send, 4 * k))
            k *= 2
        near_done.append(send)
        far_came.append(swap(send[0], 4 * k))
        done.append(keep[0])
    stay, came = finish(spots, done, far_came)
    came = swap(came, 1)
    return jnp.concatenate(
        [jnp.where(core == 0, stay, came), jnp.where(core == 0, came, stay)], axis=1
    )


def solution(mesh):
    placed = (
        P("dp", "mp"),
        P("dp", "mp"),
        P("dp", None),
        P("dp", None),
        P("mp", None),
        P(None, "dp", "mp"),
        P("mp", None),
        P("mp"),
        P("mp"),
        P("mp"),
        P("mp"),
        P("mp", None),
    )
    return jax.shard_map(
        functools.partial(local, mesh.shape["dp"], mesh.shape["mp"]),
        mesh=mesh,
        in_specs=placed,
        out_specs=P(("dp", "mp"), None),
        check_vma=False,
    )
```
